256 devices in a mesh: dp: 16 (over x_lo, y, core), tensor: 16 (over x_hi, z).
Axes of the slice: x: 4 (x_hi: 2, x_lo: 2; x = x_hi * 2 + x_lo), y: 4, z: 8, core: 2. Of those that a mesh axis runs over, the one named last changes fastest.
Arguments:
- stored: bfloat16 [896, 8192], P('tensor', 'dp'), may hold values from -6 to 6
- row_scale: float32 [896], P('tensor'), may hold values from 0.25 to 4
- out_grad: bfloat16 [896, 8192], P('tensor', 'dp'), may hold values from -1 to 1
- gate_weight: bfloat16 [8192, 28672], P('dp', 'tensor'), may hold values from -0.0625 to 0.0625
- up_weight: bfloat16 [8192, 28672], P('dp', 'tensor'), may hold values from -0.0625 to 0.0625
- down_weight: bfloat16 [28672, 8192], P('tensor', 'dp'), may hold values from -0.03125 to 0.03125
Outputs:
- grad_in: bfloat16 [896, 8192], P('tensor', 'dp')
- grad_gate: bfloat16 [8192, 28672], P('dp', 'tensor')
- grad_up: bfloat16 [8192, 28672], P('dp', 'tensor')
- grad_down: bfloat16 [28672, 8192], P('tensor', 'dp')
The draws below stay inside these ranges and needn't reach their ends.
All inputs are finite; a program needn't handle non-finite values.
Results may differ from the reference program's by a relative error of at most 0.0071.
Values may be sent and summed in bfloat16 or wider, within the bound.
A program may use at most 128 MiB of HBM per device.

```python
import math
import jax
import jax.numpy as jnp
from jax import lax

D = 8192
FF = 28672
TOKENS = 896


def steps_of(stream_key, extent, pieces, smallest, largest):
    factor_of = 1.0
    for position, shards_of in pieces:
        draws = jax.random.uniform(jax.random.fold_in(jax.random.fold_in(stream_key, 6), position), (shards_of,), jnp.float32, smallest / len(pieces), largest / len(pieces))
        factor_of = factor_of * jnp.repeat(jnp.exp(draws), extent[position] // shards_of).reshape((-1,) + (1,) * (len(extent) - 1 - position))
    return factor_of


def scatter_about(rng, extent, spread, limit, shards=(), held_as=jnp.bfloat16):
    array = jax.random.normal(rng, extent, jnp.float32) * spread
    if len(shards) > 0:
        array = steps_of(rng, extent, shards, -0.22, 0.18) * array
    return jnp.clip(array, min=-limit, max=limit).astype(held_as)


def setup_inputs(seed: int = 0) -> dict:
    seeds = jax.random.split(jax.random.key(seed), 7)
    stored = scatter_about(seeds[0], (TOKENS, D), 1.0, 6.0, ((0, 16), (1, 16)))
    row_scale = jnp.clip(jnp.exp(math.log(4.0) - 2.7725887 * jax.random.uniform(seeds[1], (TOKENS,), jnp.float32) ** steps_of(seeds[1], (TOKENS,), ((0, 16),), -0.2, 0.2)), 0.25, 4.0)
    out_grad = scatter_about(seeds[2], (TOKENS, D), 0.125, 1.0, ((0, 16), (1, 16)))
    gate_weight = scatter_about(seeds[3], (D, FF), D ** -0.5, 0.0625, ((0, 16), (1, 16)))
    up_weight = scatter_about(seeds[4], (D, FF), D ** -0.5, 0.0625, ((0, 16), (1, 16)))
    down_weight = scatter_about(seeds[5], (FF, D), FF ** -0.5, 0.03125, ((0, 16), (1, 16)))
    return dict(stored=stored, row_scale=row_scale, out_grad=out_grad, gate_weight=gate_weight, up_weight=up_weight, down_weight=down_weight)


def contract(left, right, left_dim, right_dim):
    return lax.dot_general(left, right, (((left_dim,), (right_dim,)), ((), ())), preferred_element_type=jnp.float32)


def reference(stored, row_scale, out_grad, gate_weight, up_weight, down_weight):
    inputs = (stored.astype(jnp.float32) * row_scale[:, None]).astype(jnp.bfloat16)
    gate = jnp.dot(inputs, gate_weight, preferred_element_type=jnp.float32)
    upper = jnp.dot(inputs, up_weight, preferred_element_type=jnp.float32)
    hidden_grad = contract(out_grad, down_weight, 1, 1)
    sigmoid_gate = jax.nn.sigmoid(gate)
    activated = gate * sigmoid_gate
    hidden = (activated * upper).astype(jnp.bfloat16)
    d_up = (hidden_grad * activated).astype(jnp.bfloat16)
    d_gate = (hidden_grad * upper * sigmoid_gate * (1.0 + gate * (1.0 - sigmoid_gate))).astype(jnp.bfloat16)
    grad_down = contract(hidden, out_grad, 0, 0).astype(jnp.bfloat16)
    grad_gate = contract(inputs, d_gate, 0, 0).astype(jnp.bfloat16)
    grad_up = contract(inputs, d_up, 0, 0).astype(jnp.bfloat16)
    grad_in = (contract(d_gate, gate_weight, 1, 1) + contract(d_up, up_weight, 1, 1)).astype(jnp.bfloat16)
    return (grad_in, grad_gate, grad_up, grad_down)
```

```python
import jax
import jax.numpy as jnp
from jax import lax
from jax.experimental import pallas as pl
from jax.experimental.pallas import tpu as pltpu
from jax.sharding import PartitionSpec as P

MESH = pl.DeviceIdType.MESH
BF, F32 = jnp.bfloat16, jnp.float32
COPIES = 420
FIRST = "ABABABA"


def dot(a, b):
    return lax.dot_general(a, b, (((1,), (0,)), ((), ())), preferred_element_type=F32)


def dot_t(a, b):
    return lax.dot_general(a, b, (((1,), (1,)), ((), ())), preferred_element_type=F32)


def tdot(a, b):
    return lax.dot_general(a, b, (((0,), (0,)), ((), ())), preferred_element_type=F32)


def kernel(
    own, wg, wu, wd,
    grad_in, grad_gate, grad_up, grad_down,
    blocks, x, px, xt, own_gu, own_d, peer_gu, peer_d, full_g, full_u,
    part, stage, landed, full, tile_g, tile_u, tile_d, total, tail_s, tail_r, tail_h,
    send_sem, recv_sem, load_sem,
):
    d, t = lax.axis_index("dp"), lax.axis_index("tensor")
    c, y, xl = d % 2, (d // 2) % 4, d // 8
    z, h = t % 8, t // 8
    units = part.shape[0]
    y_up, y_down, y_far = (y + 1) % 4, (y + 3) % 4, (y + 2) % 4
    peer = ((xl * 4 + y) * 2 + 1 - c, t)
    across = (((1 - xl) * 4 + y) * 2 + c, t)
    ups = ((xl * 4 + y_up) * 2 + c, t)
    downs = ((xl * 4 + y_down) * 2 + c, t)
    z_up = (d, h * 8 + (z + 1) % 8)
    z_down = (d, h * 8 + (z + 7) % 8)
    twin = (d, (1 - h) * 8 + z)
    everyone = (peer, across, ups, downs, z_up, z_down, twin)

    barrier = pltpu.get_barrier_semaphore()
    for device in everyone:
        pl.semaphore_signal(barrier, inc=1, device_id=device, device_id_type=MESH)

    index, sent, loads = {}, [], []

    def send(key, src, dst, device):
        i = index[key] = len(index)
        copy = pltpu.make_async_remote_copy(
            src_ref=src, dst_ref=dst, send_sem=send_sem.at[i], recv_sem=recv_sem.at[i],
            device_id=device, device_id_type=MESH,
        )
        copy.start()
        sent.append(copy)

    def arrive(key, dst):
        i = index[key]
        pltpu.make_async_remote_copy(
            src_ref=dst, dst_ref=dst, send_sem=send_sem.at[i], recv_sem=recv_sem.at[i],
            device_id=peer, device_id_type=MESH,
        ).wait_recv()

    def load(src, dst):
        copy = pltpu.make_async_copy(src, dst, load_sem.at[len(loads)])
        copy.start()
        loads.append(copy)
        return copy

    def cols(u, core):
        return pl.ds(pl.multiple_of(u * 256 + core * 128, 128), 128)

    own_loads = []
    for u in range(units):
        own_loads.append((
            load(wg.at[:, cols(u, c)], own_gu.at[u, :, pl.ds(0, 128)]),
            load(wu.at[:, cols(u, c)], own_gu.at[u, :, pl.ds(128, 128)]),
            load(wd.at[cols(u, c), :], own_d.at[u]),
        ))
    whole_loads = (load(wg, full_g), load(wu, full_u))
    for a in range(2):
        blocks[a, t] = own[a]

    pl.semaphore_wait(barrier, len(everyone))

    def rank(hh, zz):
        return ((h + hh) % 2) * 8 + zz

    def ring_send(a, hh, step, src_z):
        src = blocks.at[a, rank(hh, src_z)]
        return src

    far = {("+", 0): 4, ("-", 0): 3, ("+", 1): 3, ("-", 1): 4}
    for a in range(2):
        send(("+", a, 0, 1), own.at[a], blocks.at[a, t], z_up)
        send(("-", a, 0, 1), own.at[a], blocks.at[a, t], z_down)
        send(("h", a), own.at[a], blocks.at[a, t], twin)

    def peer_weights(u):
        send(("wg", u), wg.at[:, cols(u, 1 - c)], peer_gu.at[u, :, pl.ds(0, 128)], peer)
        send(("wu", u), wu.at[:, cols(u, 1 - c)], peer_gu.at[u, :, pl.ds(128, 128)], peer)
        send(("wd", u), wd.at[cols(u, 1 - c), :], peer_d.at[u], peer)

    for u in range(units):
        peer_weights(u)

    def ring_step(a, s):
        if s == 0:
            block = blocks.at[a, rank(1, z)]
            arrive(("h", a), block)
            send(("+", a, 1, 1), block, block, z_up)
            send(("-", a, 1, 1), block, block, z_down)
            return
        for hh in range(2):
            for way, device in (("+", z_up), ("-", z_down)):
                if s > far[way, hh]:
                    continue
                zz = (z + 8 - s) % 8 if way == "+" else (z + s) % 8
                block = blocks.at[a, rank(hh, zz)]
                arrive((way, a, hh, s), block)
                if s < far[way, hh]:
                    send((way, a, hh, s + 1), block, block, device)

    def repack(a):
        for k in range(8):
            rows = pl.ds(k * 112, 112)
            pair = [blocks[a, 2 * k + i].astype(F32)[:56] for i in range(2)]
            x[a, rows] = jnp.concatenate(pair, axis=0).astype(BF)
            send(("px", a, k), x.at[a, rows], px.at[a, rows], peer)

    for s in range(6):
        if s < 5:
            ring_step(0, s)
        if s == 5:
            repack(0)
        if s > 0:
            ring_step(1, s - 1)
    repack(1)
    for k in range(7):
        xt[:, k * 128 : (k + 1) * 128] = x[0, k * 128 : (k + 1) * 128].T
    for a in range(2):
        for k in range(8):
            arrive(("px", a, k), px.at[a, pl.ds(k * 112, 112)])

    def forward(u):
        for copy in own_loads[u]:
            copy.wait()
        arrive(("wg", u), peer_gu.at[u, :, pl.ds(0, 128)])
        arrive(("wu", u), peer_gu.at[u, :, pl.ds(128, 128)])
        arrive(("wd", u), peer_d.at[u])

        def rows_of(i, carry):
            rows = pl.ds(pl.multiple_of(i * 224, 224), 224)
            gu = dot(x[0, rows], own_gu[u]) + dot(px[0, rows], peer_gu[u])
            hg = dot_t(x[1, rows], own_d[u]) + dot_t(px[1, rows], peer_d[u])
            for j in range(2):
                part[u, 2 * i + j, :, 0:256] = gu[j * 112 : (j + 1) * 112]
                part[u, 2 * i + j, :, 256:384] = hg[j * 112 : (j + 1) * 112]
            return carry

        lax.fori_loop(0, 4, rows_of, 0)

    def pointwise(u, summed):
        gate, upper, grad = summed[:, :128], summed[:, 128:256], summed[:, 256:]
        sig = lax.logistic(gate)
        activated = gate * sig
        q = y * 2 + xl
        full[u, c, q, :, 0:128] = (activated * upper).astype(BF)
        full[u, c, q, :, 128:256] = (grad * upper * sig * (1.0 + gate * (1.0 - sig))).astype(BF)
        full[u, c, q, :, 256:384] = (grad * activated).astype(BF)

    def to_peer(u, q, name):
        send(("c", u, name), full.at[u, c, q], full.at[u, c, q], peer)

    def stage_a(u, s):
        st, rb = stage.at[u], landed.at[u]
        if s == 0:
            forward(u)
            for k, q, device in (
                (0, y_far * 2, ups), (1, y_far * 2 + 1, downs),
                (2, y_up * 2 + 1, ups), (3, y_down * 2, downs),
            ):
                stage[u, k] = part[u, q].astype(BF)
                send(("r", u, k), st.at[k], rb.at[k], device)
        if s == 1:
            for k, q, device in ((0, y_up * 2, ups), (1, y_down * 2 + 1, downs)):
                arrive(("r", u, k), rb.at[k])
                stage[u, 4 + k] = (part[u, q] + landed[u, k].astype(F32)).astype(BF)
                send(("r", u, 4 + k), st.at[4 + k], rb.at[4 + k], device)
        if s == 2:
            for k in (2, 3, 4, 5):
                arrive(("r", u, k), rb.at[k])
            low = part[u, 2 * y] + (landed[u, 4].astype(F32) + landed[u, 3].astype(F32))
            high = part[u, 2 * y + 1] + (landed[u, 2].astype(F32) + landed[u, 5].astype(F32))
            stage[u, 6] = jnp.where(xl == 0, high, low).astype(BF)
            send(("r", u, 6), st.at[6], rb.at[6], across)
            part[u, 2 * y + xl] = jnp.where(xl == 0, low, high)
        if s == 3:
            arrive(("r", u, 6), rb.at[6])
            pointwise(u, part[u, 2 * y + xl] + landed[u, 6].astype(F32))
            mine = full.at[u, c, 2 * y + xl]
            send(("x", u), mine, mine, across)
            send(("u", u, 0), mine, mine, ups)
            send(("d", u, 0), mine, mine, downs)
            to_peer(u, 2 * y + xl, 0)
        if s == 4:
            other = full.at[u, c, 2 * y + 1 - xl]
            arrive(("x", u), other)
            send(("u", u, 1), other, other, ups)
            send(("d", u, 1), other, other, downs)
            to_peer(u, 2 * y + 1 - xl, 1)
        if s == 5:
            for i in range(2):
                e = xl if i == 0 else 1 - xl
                arrive(("u", u, i), full.at[u, c, 2 * y_down + e])
                arrive(("d", u, i), full.at[u, c, 2 * y_up + e])
            low, high = full.at[u, c, 2 * y_down], full.at[u, c, 2 * y_up + 1]
            send(("u", u, 2), low, low, ups)
            send(("d", u, 2), high, high, downs)
            for i in range(2):
                to_peer(u, 2 * y_down + i, 2 + i)
                to_peer(u, 2 * y_up + i, 4 + i)
        if s == 6:
            arrive(("u", u, 2), full.at[u, c, 2 * y_far])
            arrive(("d", u, 2), full.at[u, c, 2 * y_far + 1])
            for i in range(2):
                to_peer(u, 2 * y_far + i, 6 + i)
        if s == 7:
            for i, q in enumerate((
                2 * y + xl, 2 * y + 1 - xl, 2 * y_down, 2 * y_down + 1,
                2 * y_up, 2 * y_up + 1, 2 * y_far, 2 * y_far + 1,
            )):
                arrive(("c", u, i), full.at[u, 1 - c, q])
            backward(u)

    lo, hi = pl.ds(0, 64), pl.ds(64, 48)

    def stage_b(u, s):
        st, rb = stage.at[u], landed.at[u]
        if s == 0:
            forward(u)
            for k, yy in enumerate((y_far, y_up, y_down, y)):
                stage[u, k] = part[u, yy * 2 + 1 - xl].astype(BF)
                send(("r", u, k), st.at[k], rb.at[k], across)
        if s == 1:
            for k, yy in enumerate((y_far, y_up, y_down, y)):
                arrive(("r", u, k), rb.at[k])
                summed = part[u, yy * 2 + xl] + landed[u, k].astype(F32)
                if k > 0:
                    part[u, yy * 2 + xl] = summed
                if k < 3:
                    stage[u, 4 + k] = summed.astype(BF)
                if k == 0:
                    send(("f", u, 0), st.at[4, lo], rb.at[4, lo], ups)
                    send(("f", u, 1), st.at[4, hi], rb.at[4, hi], downs)
                if k == 1:
                    send(("n", u, 0), st.at[5, hi], rb.at[5, hi], ups)
                if k == 2:
                    send(("n", u, 1), st.at[6, lo], rb.at[6, lo], downs)
        if s == 2:
            arrive(("f", u, 0), rb.at[4, lo])
            stage[u, 5, 0:64] = (
                part[u, y_up * 2 + xl, 0:64] + landed[u, 4, 0:64].astype(F32)
            ).astype(BF)
            send(("n", u, 2), st.at[5, lo], rb.at[5, lo], ups)
            arrive(("f", u, 1), rb.at[4, hi])
            stage[u, 6, 64:112] = (
                part[u, y_down * 2 + xl, 64:112] + landed[u, 4, 64:112].astype(F32)
            ).astype(BF)
            send(("n", u, 3), st.at[6, hi], rb.at[6, hi], downs)
        if s == 3:
            arrive(("n", u, 0), rb.at[5, hi])
            arrive(("n", u, 1), rb.at[6, lo])
            arrive(("n", u, 2), rb.at[5, lo])
            arrive(("n", u, 3), rb.at[6, hi])
            pointwise(u, part[u, 2 * y + xl] + (landed[u, 5].astype(F32) + landed[u, 6].astype(F32)))
            mine = full.at[u, c, 2 * y + xl]
            send(("u", u, 0), mine, mine, ups)
            send(("d", u, 0), mine, mine, downs)
            send(("x", u, 0), mine, mine, across)
            to_peer(u, 2 * y + xl, 0)
        if s == 4:
            low, high = full.at[u, c, 2 * y_down + xl], full.at[u, c, 2 * y_up + xl]
            arrive(("u", u, 0), low)
            send(("u", u, 1), low.at[lo], low.at[lo], ups)
            arrive(("d", u, 0), high)
            send(("d", u, 1), high.at[hi], high.at[hi], downs)
            send(("x", u, 1), low, low, across)
            send(("x", u, 2), high, high, across)
            to_peer(u, 2 * y_down + xl, 1)
            to_peer(u, 2 * y_up + xl, 2)
        if s == 5:
            opposite = full.at[u, c, 2 * y_far + xl]
            arrive(("u", u, 1), opposite.at[lo])
            arrive(("d", u, 1), opposite.at[hi])
            send(("x", u, 3), opposite, opposite, across)
            to_peer(u, 2 * y_far + xl, 3)
        order = (y, y_down, y_up, y_far)
        if s == 6:
            for i, yy in enumerate(order):
                arrive(("x", u, i), full.at[u, c, 2 * yy + 1 - xl])
                to_peer(u, 2 * yy + 1 - xl, 4 + i)
        if s == 7:
            for i, yy in enumerate(order):
                arrive(("c", u, i), full.at[u, 1 - c, 2 * yy + xl])
                arrive(("c", u, 4 + i), full.at[u, 1 - c, 2 * yy + 1 - xl])
            backward(u)

    writes = []

    def backward(u):
        wide = slice(u * 256, (u + 1) * 256)

        def lanes(k, groups=pl.ds(0, 8)):
            both = [full[u, core, groups, :, k * 128 : (k + 1) * 128] for core in range(2)]
            return jnp.concatenate([b.reshape(-1, 128) for b in both], axis=1)

        if u == 0:
            for copy in whole_loads:
                copy.wait()

        def rows_of(i, carry):
            rows = pl.ds(pl.multiple_of(i * 224, 224), 224)
            groups = pl.ds(2 * i, 2)
            term = dot_t(lanes(1, groups), full_g[:, wide]) + dot_t(lanes(2, groups), full_u[:, wide])
            total[rows] = term if u == 0 else total[rows] + term
            return carry

        lax.fori_loop(0, 4, rows_of, 0)

        def depth_of(i, carry):
            rows = pl.ds(pl.multiple_of(i * 256, 256), 256)
            tile_g[u, rows] = dot(xt[rows], lanes(1)).astype(BF)
            tile_u[u, rows] = dot(xt[rows], lanes(2)).astype(BF)
            return carry

        lax.fori_loop(0, 2, depth_of, 0)
        tile_d[u] = tdot(lanes(0), x[1]).astype(BF)
        writes.append(load(tile_g.at[u], grad_gate.at[:, pl.ds(u * 256, 256)]))
        writes.append(load(tile_u.at[u], grad_up.at[:, pl.ds(u * 256, 256)]))
        writes.append(load(tile_d.at[u], grad_down.at[pl.ds(u * 256, 256), :]))

    for tick in range(units + 7):
        for u in range(units):
            s = tick - u
            if 1 <= s <= 6:
                (stage_a if FIRST[u] == "A" else stage_b)(u, s)
        for s in (0, 7):
            u = tick - s
            if 0 <= u < units:
                (stage_a if FIRST[u] == "A" else stage_b)(u, s)

    def block_of(hh, zz):
        return total[pl.ds(pl.multiple_of((hh * 8 + zz) * 56, 8), 56)]

    def padded(value):
        return jnp.concatenate([value, jnp.zeros((8, value.shape[1]), F32)], axis=0).astype(BF)

    def tail_send(way, k, hh, add):
        device, zz = (z_up, (z + k) % 8) if way == 0 else (z_down, (z + 8 - k) % 8)
        value = block_of(hh, zz)
        if add:
            arrive(("t", way, k + 1, hh), tail_r.at[way, k, hh])
            value = value + tail_r[way, k, hh].astype(F32)[:56]
        tail_s[way, k - 1, hh] = padded(value)
        send(("t", way, k, hh), tail_s.at[way, k - 1, hh], tail_r.at[way, k - 1, hh], device)

    tail_send(0, 4, 0, False)
    tail_send(1, 4, 1, False)
    tail_send(0, 3, 1, False)
    tail_send(1, 3, 0, False)
    tail_send(0, 3, 0, True)
    tail_send(1, 3, 1, True)
    for k in (2, 1):
        for hh in ((1, 0), (0, 1)):
            for way in range(2):
                tail_send(way, k, hh[way], True)
    for hh in range(2):
        for way in range(2):
            arrive(("t", way, 1, hh), tail_r.at[way, 0, hh])

    def summed(hh):
        both = tail_r[0, 0, hh].astype(F32) + tail_r[1, 0, hh].astype(F32)
        return block_of(hh, z) + both[:56]

    tail_h[0] = padded(summed(1 - h))
    send(("twin",), tail_h.at[0], tail_h.at[1], twin)
    mine = summed(h)
    arrive(("twin",), tail_h.at[1])
    grad_in[...] = (mine + tail_h[1].astype(F32)[:56]).astype(BF)

    for copy in sent:
        copy.wait_send()
    for copy in writes:
        copy.wait()


def body(stored, row_scale, out_grad, gate_weight, up_weight, down_weight):
    tokens, depth = stored.shape
    width = gate_weight.shape[1]
    units = width // 256
    inputs = (stored.astype(F32) * row_scale[:, None]).astype(BF)
    pad = ((0, 64 - tokens), (0, 0))
    own = jnp.stack([jnp.pad(inputs, pad), jnp.pad(out_grad, pad)])
    everything = tokens * 16
    anywhere, vmem = pl.BlockSpec(memory_space=pl.ANY), pl.BlockSpec(memory_space=pltpu.VMEM)
    dma = pltpu.SemaphoreType.DMA
    return pl.pallas_call(
        kernel,
        out_shape=(
            jax.ShapeDtypeStruct((tokens, depth), BF),
            jax.ShapeDtypeStruct((depth, width), BF),
            jax.ShapeDtypeStruct((depth, width), BF),
            jax.ShapeDtypeStruct((width, depth), BF),
        ),
        in_specs=[vmem, anywhere, anywhere, anywhere],
        out_specs=(vmem, anywhere, anywhere, anywhere),
        scratch_shapes=[
            pltpu.VMEM((2, 16, 64, depth), BF),
            pltpu.VMEM((2, everything, depth), BF),
            pltpu.VMEM((2, everything, depth), BF),
            pltpu.VMEM((depth, everything), BF),
            pltpu.VMEM((units, depth, 256), BF),
            pltpu.VMEM((units, 128, depth), BF),
            pltpu.VMEM((units, depth, 256), BF),
            pltpu.VMEM((units, 128, depth), BF),
            pltpu.VMEM((depth, width), BF),
            pltpu.VMEM((depth, width), BF),
            pltpu.VMEM((units, 8, 112, 384), F32),
            pltpu.VMEM((units, 7, 112, 384), BF),
            pltpu.VMEM((units, 7, 112, 384), BF),
            pltpu.VMEM((units, 2, 8, 112, 384), BF),
            pltpu.VMEM((units, depth, 256), BF),
            pltpu.VMEM((units, depth, 256), BF),
            pltpu.VMEM((units, 256, depth), BF),
            pltpu.VMEM((everything, depth), F32),
            pltpu.VMEM((2, 4, 2, 64, depth), BF),
            pltpu.VMEM((2, 4, 2, 64, depth), BF),
            pltpu.VMEM((2, 64, depth), BF),
            dma((COPIES,)),
            dma((COPIES,)),
            dma((60,)),
        ],
        compiler_params=pltpu.CompilerParams(
            collective_id=0, has_side_effects=True, vmem_limit_bytes=62 * 2**20
        ),
        cost_estimate=pl.CostEstimate(
            flops=16 * everything * depth * width, bytes_accessed=12 * depth * width, transcendentals=0
        ),
    )(own, gate_weight, up_weight, down_weight)


def solution(mesh):
    placed = (
        P("tensor", "dp"),
        P("tensor"),
        P("tensor", "dp"),
        P("dp", "tensor"),
        P("dp", "tensor"),
        P("tensor", "dp"),
    )
    return jax.shard_map(
        body,
        mesh=mesh,
        in_specs=placed,
        out_specs=(P("tensor", "dp"), P("dp", "tensor"), P("dp", "tensor"), P("tensor", "dp")),
        check_vma=False,
    )
```

```python
import jax
import jax.numpy as jnp
from jax import lax
from jax.experimental import pallas as pl
from jax.experimental.pallas import tpu as pltpu
from jax.sharding import PartitionSpec as P

MESH = pl.DeviceIdType.MESH
BF, F32 = jnp.bfloat16, jnp.float32
COPIES = 420
FIRST = "ABABABA"
START = (0, 0, 0, 0, 0, 0, 0)
EARLY = {0: -1, 1: -1, 2: -1}
GU, HG, ALL = slice(0, 256), slice(256, 384), slice(0, 384)


def dot(a, b):
    return lax.dot_general(a, b, (((1,), (0,)), ((), ())), preferred_element_type=F32)


def dot_t(a, b):
    return lax.dot_general(a, b, (((1,), (1,)), ((), ())), preferred_element_type=F32)


def tdot(a, b):
    return lax.dot_general(a, b, (((0,), (0,)), ((), ())), preferred_element_type=F32)


def pack(value):
    half = value.shape[1] // 2
    return jnp.concatenate([value[:, :half], value[:, half:]], axis=0).astype(BF)


def unpack(block):
    value = block.astype(F32)
    rows = value.shape[0] // 2
    return jnp.concatenate([value[:rows], value[rows:]], axis=1)


def kernel(
    stored, scale, out_grad, wg, wu, wd,
    grad_in, grad_gate, grad_up, grad_down,
    blocks, twins, x, px, xt, own_d, peer_gu, peer_d, full_g, full_u,
    part, stage, landed, full, tile_g, tile_u, tile_d, total, tail_s, tail_r, tail_h,
    send_sem, recv_sem, load_sem,
):
    d, t = lax.axis_index("dp"), lax.axis_index("tensor")
    c, y, xl = d % 2, (d // 2) % 4, d // 8
    z, h = t % 8, t // 8
    units = part.shape[0]
    y_up, y_down, y_far = (y + 1) % 4, (y + 3) % 4, (y + 2) % 4
    peer = ((xl * 4 + y) * 2 + 1 - c, t)
    across = (((1 - xl) * 4 + y) * 2 + c, t)
    ups = ((xl * 4 + y_up) * 2 + c, t)
    downs = ((xl * 4 + y_down) * 2 + c, t)
    z_up = (d, h * 8 + (z + 1) % 8)
    z_down = (d, h * 8 + (z + 7) % 8)
    twin = (d, (1 - h) * 8 + z)
    z_up2 = (d, h * 8 + (z + 2) % 8)
    z_down2 = (d, h * 8 + (z + 6) % 8)
    everyone = (z_up2, z_down2, peer, across, ups, downs, z_up, z_down, twin)

    barrier = pltpu.get_barrier_semaphore()
    for device in everyone:
        pl.semaphore_signal(barrier, inc=1, device_id=device, device_id_type=MESH)

    index, sent, loads = {}, [], []

    def send(key, src, dst, device):
        i = index[key] = len(index)
        copy = pltpu.make_async_remote_copy(
            src_ref=src, dst_ref=dst, send_sem=send_sem.at[i], recv_sem=recv_sem.at[i],
            device_id=device, device_id_type=MESH,
        )
        copy.start()
        sent.append(copy)

    def arrive(key, dst):
        i = index[key]
        pltpu.make_async_remote_copy(
            src_ref=dst, dst_ref=dst, send_sem=send_sem.at[i], recv_sem=recv_sem.at[i],
            device_id=peer, device_id_type=MESH,
        ).wait_recv()

    def load(src, dst):
        copy = pltpu.make_async_copy(src, dst, load_sem.at[len(loads)])
        copy.start()
        loads.append(copy)
        return copy

    def cols(u, core):
        return pl.ds(pl.multiple_of(u * 256 + core * 128, 128), 128)

    whole_loads = (load(wg, full_g), load(wu, full_u))
    own_loads = [load(wd.at[cols(u, c), :], own_d.at[u]) for u in range(units)]
    tokens = stored.shape[0]
    same = lax.broadcasted_iota(jnp.int32, (tokens, tokens), 0) == lax.broadcasted_iota(
        jnp.int32, (tokens, tokens), 1
    )
    column = jnp.sum(jnp.where(same, scale[...], 0.0), axis=1, keepdims=True)
    blocks[0, t] = pack((stored[...].astype(F32) * column).astype(BF).astype(F32))
    blocks[1, t] = pack(out_grad[...].astype(F32))

    pl.semaphore_wait(barrier, len(everyone))

    def rank(hh, zz):
        return ((h + hh) % 2) * 8 + zz

    def block_at(a, hh, way, k):
        return blocks.at[a, rank(hh, (z + 8 - k) % 8 if way == "+" else (z + k) % 8)]

    one = {"+": z_up, "-": z_down}
    two = {"+": z_up2, "-": z_down2}
    ways = ("+", "-")
    last_way = ("+", "-")
    by_twin = [[(w, k) for k in (2, 3) for w in ways] + [(last_way[a], 4)] for a in range(2)]

    def to_other_core(a, hh, way, k):
        row = rank(hh, (z + 8 - k) % 8 if way == "+" else (z + k) % 8)
        send(("p", a, hh, way, k), blocks.at[a, row], twins.at[a, row], peer)

    def kick(a):
        block = blocks.at[a, t]
        for way in ways:
            send((1, way, a), block, block, one[way])
        send(("h", a), block, block, twin)
        for way in ways:
            send((2, way, a), block, block, two[way])
        to_other_core(a, 0, "+", 0)

    def gather_near(a):
        for way in ways:
            block = block_at(a, 0, way, 1)
            arrive((1, way, a), block)
            send((3, way, a), block, block, two[way])
            to_other_core(a, 0, way, 1)
        block = block_at(a, 1, "+", 0)
        arrive(("h", a), block)
        for way in ways:
            send(("o", way, a), block, block, one[way])
        to_other_core(a, 1, "+", 0)
        for way in ways:
            block = block_at(a, 0, way, 2)
            arrive((2, way, a), block)
            if way == last_way[a]:
                send((4, way, a), block, block, two[way])
            send(("tw", a, way, 2), block, block, twin)
            to_other_core(a, 0, way, 2)

    def gather_far(a):
        for way in ways:
            arrive(("o", way, a), block_at(a, 1, way, 1))
            to_other_core(a, 1, way, 1)
        for k in (3, 4):
            for way in ways:
                if k == 3 or way == last_way[a]:
                    block = block_at(a, 0, way, k)
                    arrive((k, way, a), block)
                    send(("tw", a, way, k), block, block, twin)
                    to_other_core(a, 0, way, k)

    def gather_last(a):
        for way, k in by_twin[a]:
            arrive(("tw", a, way, k), block_at(a, 1, way, k))
            to_other_core(a, 1, way, k)

    def repack(a):
        def move(src, dst):
            for k in range(8):
                pair = [unpack(src[a, 2 * k + i]) for i in range(2)]
                dst[a, k * 112 : (k + 1) * 112] = jnp.concatenate(pair, axis=0).astype(BF)

        move(blocks, x)
        for hh in range(2):
            for way, k in [("+", 0), ("+", 1), ("-", 1)] + by_twin[a]:
                row = rank(hh, (z + 8 - k) % 8 if way == "+" else (z + k) % 8)
                arrive(("p", a, hh, way, k), twins.at[a, row])
        move(twins, px)

    kick(0)

    def peer_weights(u):
        if u == 0:
            for copy in whole_loads:
                copy.wait()
        send(("wg", u), full_g.at[:, cols(u, 1 - c)], peer_gu.at[u, :, pl.ds(0, 128)], peer)
        send(("wu", u), full_u.at[:, cols(u, 1 - c)], peer_gu.at[u, :, pl.ds(128, 128)], peer)
        send(("wd", u), wd.at[cols(u, 1 - c), :], peer_d.at[u], peer)

    peer_weights(0)

    def transpose():
        for k in range(7):
            xt[:, k * 128 : (k + 1) * 128] = x[0, k * 128 : (k + 1) * 128].T

    gather_near(0)
    kick(1)
    gather_far(0)
    gather_near(1)
    gather_last(0)
    peer_weights(1)
    repack(0)
    gather_far(1)
    peer_weights(2)

    def forward(u, lanes):
        if lanes != HG:
            arrive(("wg", u), peer_gu.at[u, :, pl.ds(0, 128)])
            arrive(("wu", u), peer_gu.at[u, :, pl.ds(128, 128)])
        if lanes != GU:
            own_loads[u].wait()
            arrive(("wd", u), peer_d.at[u])

        def rows_of(i, carry):
            rows = pl.ds(pl.multiple_of(i * 224, 224), 224)
            if lanes != HG:
                own_gu = jnp.concatenate([full_g[:, cols(u, c)], full_u[:, cols(u, c)]], axis=1)
                gu = dot(x[0, rows], own_gu) + dot(px[0, rows], peer_gu[u])
                for j in range(2):
                    part[u, 2 * i + j, :, 0:256] = gu[j * 112 : (j + 1) * 112]
            if lanes != GU:
                hg = dot_t(x[1, rows], own_d[u]) + dot_t(px[1, rows], peer_d[u])
                for j in range(2):
                    part[u, 2 * i + j, :, 256:384] = hg[j * 112 : (j + 1) * 112]
            return carry

        lax.fori_loop(0, 4, rows_of, 0)

    def pointwise(u, summed):
        gate, upper, grad = summed[:, :128], summed[:, 128:256], summed[:, 256:]
        sig = lax.logistic(gate)
        activated = gate * sig
        q = y * 2 + xl
        full[u, c, q, :, 0:128] = (activated * upper).astype(BF)
        full[u, c, q, :, 128:256] = (grad * upper * sig * (1.0 + gate * (1.0 - sig))).astype(BF)
        full[u, c, q, :, 256:384] = (grad * activated).astype(BF)

    def finish(u, lanes, summed):
        if lanes != ALL:
            part[u, 2 * y + xl, :, lanes] = summed
        if lanes != GU:
            pointwise(u, summed if lanes == ALL else part[u, 2 * y + xl])

    def to_peer(u, q, name):
        send(("c", u, name), full.at[u, c, q], full.at[u, c, q], peer)

    def stage_a(u, s, lanes):
        st, rb, to = stage.at[u, :, :, lanes], landed.at[u, :, :, lanes], lanes.start

        def got(k):
            return landed[u, k, :, lanes].astype(F32)

        if s == 0:
            forward(u, lanes)
            for k, q, device in (
                (0, y_far * 2, ups), (1, y_far * 2 + 1, downs),
                (2, y_up * 2 + 1, ups), (3, y_down * 2, downs),
            ):
                stage[u, k, :, lanes] = part[u, q, :, lanes].astype(BF)
                send(("r", u, to, k), st.at[k], rb.at[k], device)
        if s == 1:
            for k, q, device in ((0, y_up * 2, ups), (1, y_down * 2 + 1, downs)):
                arrive(("r", u, to, k), rb.at[k])
                stage[u, 4 + k, :, lanes] = (
                    part[u, q, :, lanes] + landed[u, k, :, lanes].astype(F32)
                ).astype(BF)
                send(("r", u, to, 4 + k), st.at[4 + k], rb.at[4 + k], device)
        if s == 2:
            for k in (2, 3, 4, 5):
                arrive(("r", u, to, k), rb.at[k])
            low = part[u, 2 * y, :, lanes] + (got(4) + got(3))
            high = part[u, 2 * y + 1, :, lanes] + (got(2) + got(5))
            stage[u, 6, :, lanes] = jnp.where(xl == 0, high, low).astype(BF)
            send(("r", u, to, 6), st.at[6], rb.at[6], across)
            part[u, 2 * y + xl, :, lanes] = jnp.where(xl == 0, low, high)
        if s == 3:
            arrive(("r", u, to, 6), rb.at[6])
            finish(u, lanes, part[u, 2 * y + xl, :, lanes] + got(6))
            if lanes == GU:
                return
            mine = full.at[u, c, 2 * y + xl]
            send(("x", u), mine, mine, across)
            send(("u", u, 0), mine, mine, ups)
            send(("d", u, 0), mine, mine, downs)
            to_peer(u, 2 * y + xl, 0)
        if s == 4:
            other = full.at[u, c, 2 * y + 1 - xl]
            arrive(("x", u), other)
            send(("u", u, 1), other, other, ups)
            send(("d", u, 1), other, other, downs)
            to_peer(u, 2 * y + 1 - xl, 1)
        if s == 5:
            for i in range(2):
                e = xl if i == 0 else 1 - xl
                arrive(("u", u, i), full.at[u, c, 2 * y_down + e])
                arrive(("d", u, i), full.at[u, c, 2 * y_up + e])
            low, high = full.at[u, c, 2 * y_down], full.at[u, c, 2 * y_up + 1]
            send(("u", u, 2), low, low, ups)
            send(("d", u, 2), high, high, downs)
            for i in range(2):
                to_peer(u, 2 * y_down + i, 2 + i)
                to_peer(u, 2 * y_up + i, 4 + i)
        if s == 6:
            arrive(("u", u, 2), full.at[u, c, 2 * y_far])
            arrive(("d", u, 2), full.at[u, c, 2 * y_far + 1])
            for i in range(2):
                to_peer(u, 2 * y_far + i, 6 + i)
        if s == 7:
            for i, q in enumerate((
                2 * y + xl, 2 * y + 1 - xl, 2 * y_down, 2 * y_down + 1,
                2 * y_up, 2 * y_up + 1, 2 * y_far, 2 * y_far + 1,
            )):
                arrive(("c", u, i), full.at[u, 1 - c, q])
            backward(u)

    lo, hi = pl.ds(0, 64), pl.ds(64, 48)

    def stage_b(u, s, lanes):
        st, rb, to = stage.at[u, :, :, lanes], landed.at[u, :, :, lanes], lanes.start
        if s == 0:
            forward(u, lanes)
            for k, yy in enumerate((y_far, y_up, y_down, y)):
                stage[u, k, :, lanes] = part[u, yy * 2 + 1 - xl, :, lanes].astype(BF)
                send(("r", u, to, k), st.at[k], rb.at[k], across)
        if s == 1:
            for k, yy in enumerate((y_far, y_up, y_down, y)):
                arrive(("r", u, to, k), rb.at[k])
                summed = part[u, yy * 2 + xl, :, lanes] + landed[u, k, :, lanes].astype(F32)
                if k > 0:
                    part[u, yy * 2 + xl, :, lanes] = summed
                if k < 3:
                    stage[u, 4 + k, :, lanes] = summed.astype(BF)
                if k == 0:
                    send(("f", u, to, 0), st.at[4, lo], rb.at[4, lo], ups)
                    send(("f", u, to, 1), st.at[4, hi], rb.at[4, hi], downs)
                if k == 1:
                    send(("n", u, to, 0), st.at[5, hi], rb.at[5, hi], ups)
                if k == 2:
                    send(("n", u, to, 1), st.at[6, lo], rb.at[6, lo], downs)
        if s == 2:
            arrive(("f", u, to, 0), rb.at[4, lo])
            stage[u, 5, 0:64, lanes] = (
                part[u, y_up * 2 + xl, 0:64, lanes] + landed[u, 4, 0:64, lanes].astype(F32)
            ).astype(BF)
            send(("n", u, to, 2), st.at[5, lo], rb.at[5, lo], ups)
            arrive(("f", u, to, 1), rb.at[4, hi])
            stage[u, 6, 64:112, lanes] = (
                part[u, y_down * 2 + xl, 64:112, lanes] + landed[u, 4, 64:112, lanes].astype(F32)
            ).astype(BF)
            send(("n", u, to, 3), st.at[6, hi], rb.at[6, hi], downs)
        if s == 3:
            arrive(("n", u, to, 0), rb.at[5, hi])
            arrive(("n", u, to, 1), rb.at[6, lo])
            arrive(("n", u, to, 2), rb.at[5, lo])
            arrive(("n", u, to, 3), rb.at[6, hi])
            both = landed[u, 5, :, lanes].astype(F32) + landed[u, 6, :, lanes].astype(F32)
            finish(u, lanes, part[u, 2 * y + xl, :, lanes] + both)
            if lanes == GU:
                return
            mine = full.at[u, c, 2 * y + xl]
            send(("u", u, 0), mine, mine, ups)
            send(("d", u, 0), mine, mine, downs)
            send(("x", u, 0), mine, mine, across)
            to_peer(u, 2 * y + xl, 0)
        if s == 4:
            low, high = full.at[u, c, 2 * y_down + xl], full.at[u, c, 2 * y_up + xl]
            arrive(("u", u, 0), low)
            send(("u", u, 1), low.at[lo], low.at[lo], ups)
            arrive(("d", u, 0), high)
            send(("d", u, 1), high.at[hi], high.at[hi], downs)
            send(("x", u, 1), low, low, across)
            send(("x", u, 2), high, high, across)
            to_peer(u, 2 * y_down + xl, 1)
            to_peer(u, 2 * y_up + xl, 2)
        if s == 5:
            opposite = full.at[u, c, 2 * y_far + xl]
            arrive(("u", u, 1), opposite.at[lo])
            arrive(("d", u, 1), opposite.at[hi])
            send(("x", u, 3), opposite, opposite, across)
            to_peer(u, 2 * y_far + xl, 3)
        order = (y, y_down, y_up, y_far)
        if s == 6:
            for i, yy in enumerate(order):
                arrive(("x", u, i), full.at[u, c, 2 * yy + 1 - xl])
                to_peer(u, 2 * yy + 1 - xl, 4 + i)
        if s == 7:
            for i, yy in enumerate(order):
                arrive(("c", u, i), full.at[u, 1 - c, 2 * yy + xl])
                arrive(("c", u, 4 + i), full.at[u, 1 - c, 2 * yy + 1 - xl])
            backward(u)

    writes = []

    def backward(u):
        wide = slice(u * 256, (u + 1) * 256)

        def lanes(k, groups=pl.ds(0, 8)):
            both = [full[u, core, groups, :, k * 128 : (k + 1) * 128] for core in range(2)]
            return jnp.concatenate([b.reshape(-1, 128) for b in both], axis=1)

        def rows_of(i, carry):
            rows = pl.ds(pl.multiple_of(i * 224, 224), 224)
            groups = pl.ds(2 * i, 2)
            term = dot_t(lanes(1, groups), full_g[:, wide]) + dot_t(lanes(2, groups), full_u[:, wide])
            total[rows] = term if u == 0 else total[rows] + term
            return carry

        lax.fori_loop(0, 4, rows_of, 0)

        def depth_of(i, carry):
            rows = pl.ds(pl.multiple_of(i * 256, 256), 256)
            tile_g[u, rows] = dot(xt[rows], lanes(1)).astype(BF)
            tile_u[u, rows] = dot(xt[rows], lanes(2)).astype(BF)
            return carry

        lax.fori_loop(0, 2, depth_of, 0)
        tile_d[u] = tdot(lanes(0), x[1]).astype(BF)
        writes.append(load(tile_g.at[u], grad_gate.at[:, pl.ds(u * 256, 256)]))
        writes.append(load(tile_u.at[u], grad_up.at[:, pl.ds(u * 256, 256)]))
        writes.append(load(tile_d.at[u], grad_down.at[pl.ds(u * 256, 256), :]))

    def act(u, s, lanes):
        (stage_a if FIRST[u] == "A" else stage_b)(u, s, lanes)

    first_tick = min(EARLY.values(), default=0)
    for tick in range(first_tick, max(START) + 8):
        if tick == 0:
            gather_last(1)
            for u in range(3, units):
                peer_weights(u)
            repack(1)
        works = [(tick - START[u], u, HG if u in EARLY else ALL) for u in range(units)]
        works += [(tick - EARLY[u], u, GU) for u in EARLY if tick - EARLY[u] <= 3]
        for s, u, lanes in sorted(works, key=lambda w: (-w[0], w[1], w[2].start)):
            if 1 <= s <= 6:
                act(u, s, lanes)
        for want in (0, 7):
            for s, u, lanes in works:
                if s == want:
                    act(u, s, lanes)
        if tick == first_tick:
            transpose()

    def block_of(hh, zz):
        return total[pl.ds(pl.multiple_of((hh * 8 + zz) * 56, 8), 56)]

    def tail_send(way, k, hh, add):
        device, zz = (z_up, (z + k) % 8) if way == 0 else (z_down, (z + 8 - k) % 8)
        value = block_of(hh, zz)
        if add:
            arrive(("t", way, k + 1, hh), tail_r.at[way, k, hh])
            value = value + unpack(tail_r[way, k, hh])
        tail_s[way, k - 1, hh] = pack(value)
        send(("t", way, k, hh), tail_s.at[way, k - 1, hh], tail_r.at[way, k - 1, hh], device)

    tail_send(0, 4, 0, False)
    tail_send(1, 4, 1, False)
    tail_send(0, 3, 1, False)
    tail_send(1, 3, 0, False)
    tail_send(0, 3, 0, True)
    tail_send(1, 3, 1, True)
    for k in (2, 1):
        for hh in ((1, 0), (0, 1)):
            for way in range(2):
                tail_send(way, k, hh[way], True)
    for hh in range(2):
        for way in range(2):
            arrive(("t", way, 1, hh), tail_r.at[way, 0, hh])

    def summed(hh):
        return block_of(hh, z) + (unpack(tail_r[0, 0, hh]) + unpack(tail_r[1, 0, hh]))

    tail_h[0] = pack(summed(1 - h))
    send(("twin",), tail_h.at[0], tail_h.at[1], twin)
    mine = summed(h)
    arrive(("twin",), tail_h.at[1])
    grad_in[...] = (mine + unpack(tail_h[1])).astype(BF)

    for copy in sent:
        copy.wait_send()
    for copy in writes:
        copy.wait()


def hand_over(*refs):
    srcs, dsts, held, sem = refs[:4], refs[4:8], refs[8:12], refs[12]
    moves = []
    for i in range(4):
        pieces = 4 if i > 0 else 1
        rows = srcs[i].shape[0] // pieces
        for j in range(pieces):
            at = pl.ds(j * rows, rows)
            moves.append((
                pltpu.make_async_copy(srcs[i].at[at], held[i].at[at], sem.at[0, i, j]),
                pltpu.make_async_copy(held[i].at[at], dsts[i].at[at], sem.at[1, i, j]),
            ))
    for get, _ in moves:
        get.start()
    for get, put in moves:
        get.wait()
        put.start()
    for _, put in moves:
        put.wait()


def body(stored, row_scale, out_grad, gate_weight, up_weight, down_weight):
    tokens, depth = stored.shape
    width = gate_weight.shape[1]
    units = width // 256
    narrow = (112, depth // 2)
    everything = tokens * 16
    anywhere, vmem = pl.BlockSpec(memory_space=pl.ANY), pl.BlockSpec(memory_space=pltpu.VMEM)
    dma = pltpu.SemaphoreType.DMA
    grads = pl.pallas_call(
        kernel,
        out_shape=(
            jax.ShapeDtypeStruct((tokens, depth), BF),
            jax.ShapeDtypeStruct((depth, width), BF),
            jax.ShapeDtypeStruct((depth, width), BF),
            jax.ShapeDtypeStruct((width, depth), BF),
        ),
        in_specs=[vmem, vmem, vmem, anywhere, anywhere, anywhere],
        out_specs=(vmem, anywhere, anywhere, anywhere),
        scratch_shapes=[
            pltpu.VMEM((2, 16, *narrow), BF),
            pltpu.VMEM((2, 16, *narrow), BF),
            pltpu.VMEM((2, everything, depth), BF),
            pltpu.VMEM((2, everything, depth), BF),
            pltpu.VMEM((depth, everything), BF),
            pltpu.VMEM((units, 128, depth), BF),
            pltpu.VMEM((units, depth, 256), BF),
            pltpu.VMEM((units, 128, depth), BF),
            pltpu.VMEM((depth, width), BF),
            pltpu.VMEM((depth, width), BF),
            pltpu.VMEM((units, 8, 112, 384), F32),
            pltpu.VMEM((units, 7, 112, 384), BF),
            pltpu.VMEM((units, 7, 112, 384), BF),
            pltpu.VMEM((units, 2, 8, 112, 384), BF),
            pltpu.VMEM((units, depth, 256), BF),
            pltpu.VMEM((units, depth, 256), BF),
            pltpu.VMEM((units, 256, depth), BF),
            pltpu.VMEM((everything, depth), F32),
            pltpu.VMEM((2, 4, 2, *narrow), BF),
            pltpu.VMEM((2, 4, 2, *narrow), BF),
            pltpu.VMEM((2, *narrow), BF),
            dma((COPIES,)),
            dma((COPIES,)),
            dma((60,)),
        ],
        compiler_params=pltpu.CompilerParams(
            collective_id=0, has_side_effects=True, vmem_limit_bytes=62 * 2**20
        ),
        cost_estimate=pl.CostEstimate(
            flops=16 * everything * depth * width, bytes_accessed=12 * depth * width, transcendentals=0
        ),
    )(stored, row_scale[None, :], out_grad, gate_weight, up_weight, down_weight)
    return pl.pallas_call(
        hand_over,
        out_shape=tuple(jax.ShapeDtypeStruct(g.shape, g.dtype) for g in grads),
        in_specs=[anywhere] * 4,
        out_specs=(anywhere,) * 4,
        scratch_shapes=[pltpu.VMEM(g.shape, g.dtype) for g in grads] + [dma((2, 4, 4))],
        compiler_params=pltpu.CompilerParams(vmem_limit_bytes=62 * 2**20),
    )(*grads)


def solution(mesh):
    placed = (
        P("tensor", "dp"),
        P("tensor"),
        P("tensor", "dp"),
        P("dp", "tensor"),
        P("dp", "tensor"),
        P("tensor", "dp"),
    )
    return jax.shard_map(
        body,
        mesh=mesh,
        in_specs=placed,
        out_specs=(P("tensor", "dp"), P("dp", "tensor"), P("dp", "tensor"), P("tensor", "dp")),
        check_vma=False,
    )
```

```python
import jax
import jax.numpy as jnp
from jax import lax
from jax.experimental import pallas as pl
from jax.experimental.pallas import tpu as pltpu
from jax.sharding import PartitionSpec as P

MESH = pl.DeviceIdType.MESH
BF, F32 = jnp.bfloat16, jnp.float32
COPIES = 420
FIRST = "ABABABA"
START = (0, 0, 0, 0, 0, 0, 0)
BEHIND = 2
EARLY = {0: -1, 1: -1, 2: -1}
GU, HG, ALL = slice(0, 256), slice(256, 384), slice(0, 384)


def dot(a, b):
    return lax.dot_general(a, b, (((1,), (0,)), ((), ())), preferred_element_type=F32)


def dot_t(a, b):
    return lax.dot_general(a, b, (((1,), (1,)), ((), ())), preferred_element_type=F32)


def tdot(a, b):
    return lax.dot_general(a, b, (((0,), (0,)), ((), ())), preferred_element_type=F32)


def pack(value):
    half = value.shape[1] // 2
    return jnp.concatenate([value[:, :half], value[:, half:]], axis=0).astype(BF)


def unpack(block):
    value = block.astype(F32)
    rows = value.shape[0] // 2
    return jnp.concatenate([value[:rows], value[rows:]], axis=1)


def kernel(
    stored, scale, out_grad, wg, wu, wd,
    grad_in, grad_gate, grad_up, grad_down,
    blocks, twins, x, px, xt, own_d, peer_gu, peer_d, full_g, full_u,
    part, stage, landed, full, tile_g, tile_u, tile_d, total, tail_s, tail_r, tail_h,
    send_sem, recv_sem, load_sem,
):
    d, t = lax.axis_index("dp"), lax.axis_index("tensor")
    c, y, xl = d % 2, (d // 2) % 4, d // 8
    z, h = t % 8, t // 8
    units = part.shape[0]
    y_up, y_down, y_far = (y + 1) % 4, (y + 3) % 4, (y + 2) % 4
    peer = ((xl * 4 + y) * 2 + 1 - c, t)
    across = (((1 - xl) * 4 + y) * 2 + c, t)
    ups = ((xl * 4 + y_up) * 2 + c, t)
    downs = ((xl * 4 + y_down) * 2 + c, t)
    z_up = (d, h * 8 + (z + 1) % 8)
    z_down = (d, h * 8 + (z + 7) % 8)
    twin = (d, (1 - h) * 8 + z)
    z_up2 = (d, h * 8 + (z + 2) % 8)
    z_down2 = (d, h * 8 + (z + 6) % 8)
    everyone = (z_up2, z_down2, peer, across, ups, downs, z_up, z_down, twin)

    barrier = pltpu.get_barrier_semaphore()
    for device in everyone:
        pl.semaphore_signal(barrier, inc=1, device_id=device, device_id_type=MESH)

    index, sent, loads = {}, [], []

    def send(key, src, dst, device):
        i = index[key] = len(index)
        copy = pltpu.make_async_remote_copy(
            src_ref=src, dst_ref=dst, send_sem=send_sem.at[i], recv_sem=recv_sem.at[i],
            device_id=device, device_id_type=MESH,
        )
        copy.start()
        sent.append(copy)

    def arrive(key, dst):
        i = index[key]
        pltpu.make_async_remote_copy(
            src_ref=dst, dst_ref=dst, send_sem=send_sem.at[i], recv_sem=recv_sem.at[i],
            device_id=peer, device_id_type=MESH,
        ).wait_recv()

    def load(src, dst):
        copy = pltpu.make_async_copy(src, dst, load_sem.at[len(loads)])
        copy.start()
        loads.append(copy)
        return copy

    def cols(u, core):
        return pl.ds(pl.multiple_of(u * 256 + core * 128, 128), 128)

    whole_loads = (load(wg, full_g), load(wu, full_u))
    own_loads = [load(wd.at[cols(u, c), :], own_d.at[u]) for u in range(units)]
    tokens = stored.shape[0]
    same = lax.broadcasted_iota(jnp.int32, (tokens, tokens), 0) == lax.broadcasted_iota(
        jnp.int32, (tokens, tokens), 1
    )
    column = jnp.sum(jnp.where(same, scale[...], 0.0), axis=1, keepdims=True)
    blocks[0, t] = pack((stored[...].astype(F32) * column).astype(BF).astype(F32))
    blocks[1, t] = pack(out_grad[...].astype(F32))

    pl.semaphore_wait(barrier, len(everyone))

    def rank(hh, zz):
        return ((h + hh) % 2) * 8 + zz

    def block_at(a, hh, way, k):
        return blocks.at[a, rank(hh, (z + 8 - k) % 8 if way == "+" else (z + k) % 8)]

    one = {"+": z_up, "-": z_down}
    two = {"+": z_up2, "-": z_down2}
    ways = ("+", "-")
    last_way = ("+", "-")
    by_twin = [[(w, k) for k in (2, 3) for w in ways] + [(last_way[a], 4)] for a in range(2)]

    def to_other_core(a, hh, way, k):
        row = rank(hh, (z + 8 - k) % 8 if way == "+" else (z + k) % 8)
        send(("p", a, hh, way, k), blocks.at[a, row], twins.at[a, row], peer)

    def kick(a):
        block = blocks.at[a, t]
        for way in ways:
            send((1, way, a), block, block, one[way])
        send(("h", a), block, block, twin)
        for way in ways:
            send((2, way, a), block, block, two[way])
        to_other_core(a, 0, "+", 0)

    def gather_near(a):
        for way in ways:
            block = block_at(a, 0, way, 1)
            arrive((1, way, a), block)
            send((3, way, a), block, block, two[way])
            to_other_core(a, 0, way, 1)
        block = block_at(a, 1, "+", 0)
        arrive(("h", a), block)
        for way in ways:
            send(("o", way, a), block, block, one[way])
        to_other_core(a, 1, "+", 0)
        for way in ways:
            block = block_at(a, 0, way, 2)
            arrive((2, way, a), block)
            if way == last_way[a]:
                send((4, way, a), block, block, two[way])
            send(("tw", a, way, 2), block, block, twin)
            to_other_core(a, 0, way, 2)

    def gather_far(a):
        for way in ways:
            arrive(("o", way, a), block_at(a, 1, way, 1))
            to_other_core(a, 1, way, 1)
        for k in (3, 4):
            for way in ways:
                if k == 3 or way == last_way[a]:
                    block = block_at(a, 0, way, k)
                    arrive((k, way, a), block)
                    send(("tw", a, way, k), block, block, twin)
                    to_other_core(a, 0, way, k)

    def gather_last(a):
        for way, k in by_twin[a]:
            arrive(("tw", a, way, k), block_at(a, 1, way, k))
            to_other_core(a, 1, way, k)

    def repack(a):
        def move(src, dst):
            for k in range(8):
                pair = [unpack(src[a, 2 * k + i]) for i in range(2)]
                dst[a, k * 112 : (k + 1) * 112] = jnp.concatenate(pair, axis=0).astype(BF)

        move(blocks, x)
        for hh in range(2):
            for way, k in [("+", 0), ("+", 1), ("-", 1)] + by_twin[a]:
                row = rank(hh, (z + 8 - k) % 8 if way == "+" else (z + k) % 8)
                arrive(("p", a, hh, way, k), twins.at[a, row])
        move(twins, px)

    kick(0)

    def peer_weights(u):
        if u == 0:
            for copy in whole_loads:
                copy.wait()
        send(("wg", u), full_g.at[:, cols(u, 1 - c)], peer_gu.at[u, :, pl.ds(0, 128)], peer)
        send(("wu", u), full_u.at[:, cols(u, 1 - c)], peer_gu.at[u, :, pl.ds(128, 128)], peer)
        send(("wd", u), wd.at[cols(u, 1 - c), :], peer_d.at[u], peer)

    peer_weights(0)

    def transpose():
        for k in range(7):
            xt[:, k * 128 : (k + 1) * 128] = x[0, k * 128 : (k + 1) * 128].T

    gather_near(0)
    kick(1)
    gather_far(0)
    gather_near(1)
    gather_last(0)
    peer_weights(1)
    repack(0)
    gather_far(1)
    peer_weights(2)

    def forward(u, lanes):
        if lanes != HG:
            arrive(("wg", u), peer_gu.at[u, :, pl.ds(0, 128)])
            arrive(("wu", u), peer_gu.at[u, :, pl.ds(128, 128)])
        if lanes != GU:
            own_loads[u].wait()
            arrive(("wd", u), peer_d.at[u])

        def rows_of(i, carry):
            rows = pl.ds(pl.multiple_of(i * 224, 224), 224)
            if lanes != HG:
                own_gu = jnp.concatenate([full_g[:, cols(u, c)], full_u[:, cols(u, c)]], axis=1)
                gu = dot(x[0, rows], own_gu) + dot(px[0, rows], peer_gu[u])
                for j in range(2):
                    part[u, 2 * i + j, :, 0:256] = gu[j * 112 : (j + 1) * 112]
            if lanes != GU:
                hg = dot_t(x[1, rows], own_d[u]) + dot_t(px[1, rows], peer_d[u])
                for j in range(2):
                    part[u, 2 * i + j, :, 256:384] = hg[j * 112 : (j + 1) * 112]
            return carry

        lax.fori_loop(0, 4, rows_of, 0)

    def pointwise(u, summed):
        gate, upper, grad = summed[:, :128], summed[:, 128:256], summed[:, 256:]
        sig = lax.logistic(gate)
        activated = gate * sig
        q = y * 2 + xl
        full[u, c, q, :, 0:128] = (activated * upper).astype(BF)
        full[u, c, q, :, 128:256] = (grad * upper * sig * (1.0 + gate * (1.0 - sig))).astype(BF)
        full[u, c, q, :, 256:384] = (grad * activated).astype(BF)

    def finish(u, lanes, summed):
        if lanes != ALL:
            part[u, 2 * y + xl, :, lanes] = summed
        if lanes != GU:
            pointwise(u, summed if lanes == ALL else part[u, 2 * y + xl])

    def to_peer(u, q, name):
        send(("c", u, name), full.at[u, c, q], full.at[u, c, q], peer)

    def stage_a(u, s, lanes):
        st, rb, to = stage.at[u, :, :, lanes], landed.at[u, :, :, lanes], lanes.start

        def got(k):
            return landed[u, k, :, lanes].astype(F32)

        if s == 0:
            forward(u, lanes)
            for k, q, device in (
                (0, y_far * 2, ups), (1, y_far * 2 + 1, downs),
                (2, y_up * 2 + 1, ups), (3, y_down * 2, downs),
            ):
                stage[u, k, :, lanes] = part[u, q, :, lanes].astype(BF)
                send(("r", u, to, k), st.at[k], rb.at[k], device)
        if s == 1:
            for k, q, device in ((0, y_up * 2, ups), (1, y_down * 2 + 1, downs)):
                arrive(("r", u, to, k), rb.at[k])
                stage[u, 4 + k, :, lanes] = (
                    part[u, q, :, lanes] + landed[u, k, :, lanes].astype(F32)
                ).astype(BF)
                send(("r", u, to, 4 + k), st.at[4 + k], rb.at[4 + k], device)
        if s == 2:
            for k in (2, 3, 4, 5):
                arrive(("r", u, to, k), rb.at[k])
            low = part[u, 2 * y, :, lanes] + (got(4) + got(3))
            high = part[u, 2 * y + 1, :, lanes] + (got(2) + got(5))
            stage[u, 6, :, lanes] = jnp.where(xl == 0, high, low).astype(BF)
            send(("r", u, to, 6), st.at[6], rb.at[6], across)
            part[u, 2 * y + xl, :, lanes] = jnp.where(xl == 0, low, high)
        if s == 3:
            arrive(("r", u, to, 6), rb.at[6])
            finish(u, lanes, part[u, 2 * y + xl, :, lanes] + got(6))
            if lanes == GU:
                return
            mine = full.at[u, c, 2 * y + xl]
            send(("x", u), mine, mine, across)
            send(("u", u, 0), mine, mine, ups)
            send(("d", u, 0), mine, mine, downs)
            to_peer(u, 2 * y + xl, 0)
        if s == 4:
            other = full.at[u, c, 2 * y + 1 - xl]
            arrive(("x", u), other)
            send(("u", u, 1), other, other, ups)
            send(("d", u, 1), other, other, downs)
            to_peer(u, 2 * y + 1 - xl, 1)
        if s == 5:
            for i in range(2):
                e = xl if i == 0 else 1 - xl
                arrive(("u", u, i), full.at[u, c, 2 * y_down + e])
                arrive(("d", u, i), full.at[u, c, 2 * y_up + e])
            low, high = full.at[u, c, 2 * y_down], full.at[u, c, 2 * y_up + 1]
            send(("u", u, 2), low, low, ups)
            send(("d", u, 2), high, high, downs)
            for i in range(2):
                to_peer(u, 2 * y_down + i, 2 + i)
                to_peer(u, 2 * y_up + i, 4 + i)
        if s == 6:
            arrive(("u", u, 2), full.at[u, c, 2 * y_far])
            arrive(("d", u, 2), full.at[u, c, 2 * y_far + 1])
            for i in range(2):
                to_peer(u, 2 * y_far + i, 6 + i)
        if s == 7:
            for i, q in enumerate((
                2 * y + xl, 2 * y + 1 - xl, 2 * y_down, 2 * y_down + 1,
                2 * y_up, 2 * y_up + 1, 2 * y_far, 2 * y_far + 1,
            )):
                arrive(("c", u, i), full.at[u, 1 - c, q])
            backward(u)

    lo, hi = pl.ds(0, 64), pl.ds(64, 48)

    def stage_b(u, s, lanes):
        st, rb, to = stage.at[u, :, :, lanes], landed.at[u, :, :, lanes], lanes.start
        if s == 0:
            forward(u, lanes)
            for k, yy in enumerate((y_far, y_up, y_down, y)):
                stage[u, k, :, lanes] = part[u, yy * 2 + 1 - xl, :, lanes].astype(BF)
                send(("r", u, to, k), st.at[k], rb.at[k], across)
        if s == 1:
            for k, yy in enumerate((y_far, y_up, y_down, y)):
                arrive(("r", u, to, k), rb.at[k])
                summed = part[u, yy * 2 + xl, :, lanes] + landed[u, k, :, lanes].astype(F32)
                if k > 0:
                    part[u, yy * 2 + xl, :, lanes] = summed
                if k < 3:
                    stage[u, 4 + k, :, lanes] = summed.astype(BF)
                if k == 0:
                    send(("f", u, to, 0), st.at[4, lo], rb.at[4, lo], ups)
                    send(("f", u, to, 1), st.at[4, hi], rb.at[4, hi], downs)
                if k == 1:
                    send(("n", u, to, 0), st.at[5, hi], rb.at[5, hi], ups)
                if k == 2:
                    send(("n", u, to, 1), st.at[6, lo], rb.at[6, lo], downs)
        if s == 2:
            arrive(("f", u, to, 0), rb.at[4, lo])
            stage[u, 5, 0:64, lanes] = (
                part[u, y_up * 2 + xl, 0:64, lanes] + landed[u, 4, 0:64, lanes].astype(F32)
            ).astype(BF)
            send(("n", u, to, 2), st.at[5, lo], rb.at[5, lo], ups)
            arrive(("f", u, to, 1), rb.at[4, hi])
            stage[u, 6, 64:112, lanes] = (
                part[u, y_down * 2 + xl, 64:112, lanes] + landed[u, 4, 64:112, lanes].astype(F32)
            ).astype(BF)
            send(("n", u, to, 3), st.at[6, hi], rb.at[6, hi], downs)
        if s == 3:
            arrive(("n", u, to, 0), rb.at[5, hi])
            arrive(("n", u, to, 1), rb.at[6, lo])
            arrive(("n", u, to, 2), rb.at[5, lo])
            arrive(("n", u, to, 3), rb.at[6, hi])
            both = landed[u, 5, :, lanes].astype(F32) + landed[u, 6, :, lanes].astype(F32)
            finish(u, lanes, part[u, 2 * y + xl, :, lanes] + both)
            if lanes == GU:
                return
            mine = full.at[u, c, 2 * y + xl]
            send(("u", u, 0), mine, mine, ups)
            send(("d", u, 0), mine, mine, downs)
            send(("x", u, 0), mine, mine, across)
            to_peer(u, 2 * y + xl, 0)
        if s == 4:
            low, high = full.at[u, c, 2 * y_down + xl], full.at[u, c, 2 * y_up + xl]
            arrive(("u", u, 0), low)
            send(("u", u, 1), low.at[lo], low.at[lo], ups)
            arrive(("d", u, 0), high)
            send(("d", u, 1), high.at[hi], high.at[hi], downs)
            send(("x", u, 1), low, low, across)
            send(("x", u, 2), high, high, across)
            to_peer(u, 2 * y_down + xl, 1)
            to_peer(u, 2 * y_up + xl, 2)
        if s == 5:
            opposite = full.at[u, c, 2 * y_far + xl]
            arrive(("u", u, 1), opposite.at[lo])
            arrive(("d", u, 1), opposite.at[hi])
            send(("x", u, 3), opposite, opposite, across)
            to_peer(u, 2 * y_far + xl, 3)
        order = (y, y_down, y_up, y_far)
        if s == 6:
            for i, yy in enumerate(order):
                arrive(("x", u, i), full.at[u, c, 2 * yy + 1 - xl])
                to_peer(u, 2 * yy + 1 - xl, 4 + i)
        if s == 7:
            for i, yy in enumerate(order):
                arrive(("c", u, i), full.at[u, 1 - c, 2 * yy + xl])
                arrive(("c", u, 4 + i), full.at[u, 1 - c, 2 * yy + 1 - xl])
            backward(u)

    writes = []

    def backward(u):
        wide = slice(u * 256, (u + 1) * 256)

        def lanes(k, groups=pl.ds(0, 8)):
            both = [full[u, core, groups, :, k * 128 : (k + 1) * 128] for core in range(2)]
            return jnp.concatenate([b.reshape(-1, 128) for b in both], axis=1)

        def rows_of(i, carry):
            rows = pl.ds(pl.multiple_of(i * 224, 224), 224)
            groups = pl.ds(2 * i, 2)
            term = dot_t(lanes(1, groups), full_g[:, wide]) + dot_t(lanes(2, groups), full_u[:, wide])
            total[rows] = term if u == 0 else total[rows] + term
            return carry

        lax.fori_loop(0, 4, rows_of, 0)

    def weight_grads(u):
        def lanes(k):
            both = [full[u, core, :, :, k * 128 : (k + 1) * 128] for core in range(2)]
            return jnp.concatenate([b.reshape(-1, 128) for b in both], axis=1)

        def depth_of(i, carry):
            rows = pl.ds(pl.multiple_of(i * 256, 256), 256)
            tile_g[u, rows] = dot(xt[rows], lanes(1)).astype(BF)
            tile_u[u, rows] = dot(xt[rows], lanes(2)).astype(BF)
            return carry

        lax.fori_loop(0, 2, depth_of, 0)
        tile_d[u] = tdot(lanes(0), x[1]).astype(BF)
        writes.append(load(tile_g.at[u], grad_gate.at[:, pl.ds(u * 256, 256)]))
        writes.append(load(tile_u.at[u], grad_up.at[:, pl.ds(u * 256, 256)]))
        writes.append(load(tile_d.at[u], grad_down.at[pl.ds(u * 256, 256), :]))

    def act(u, s, lanes):
        (stage_a if FIRST[u] == "A" else stage_b)(u, s, lanes)

    first_tick = min(EARLY.values(), default=0)
    for tick in range(first_tick, max(START) + 7):
        if tick == 0:
            gather_last(1)
            for u in range(3, units):
                peer_weights(u)
            repack(1)
        works = [(tick - START[u], u, HG if u in EARLY else ALL) for u in range(units)]
        works += [(tick - EARLY[u], u, GU) for u in EARLY if tick - EARLY[u] <= 3]
        for s, u, lanes in sorted(works, key=lambda w: (-w[0], w[1], w[2].start)):
            if 1 <= s <= 6:
                act(u, s, lanes)
            if s == 6 and u >= BEHIND:
                act(u - BEHIND, 7, ALL)
                if u - BEHIND < units - 4:
                    weight_grads(u - BEHIND)
        for s, u, lanes in works:
            if s == 0:
                act(u, s, lanes)
        if tick == 0:
            transpose()
    for u in range(units - BEHIND, units):
        act(u, 7, ALL)

    def block_of(hh, zz):
        return total[pl.ds(pl.multiple_of((hh * 8 + zz) * 56, 8), 56)]

    def tail_send(way, k, hh, add):
        device, zz = (z_up, (z + k) % 8) if way == 0 else (z_down, (z + 8 - k) % 8)
        value = block_of(hh, zz)
        if add:
            arrive(("t", way, k + 1, hh), tail_r.at[way, k, hh])
            value = value + unpack(tail_r[way, k, hh])
        tail_s[way, k - 1, hh] = pack(value)
        send(("t", way, k, hh), tail_s.at[way, k - 1, hh], tail_r.at[way, k - 1, hh], device)

    tail_send(0, 4, 0, False)
    tail_send(1, 4, 1, False)
    tail_send(0, 3, 1, False)
    tail_send(1, 3, 0, False)
    weight_grads(units - 4)
    tail_send(0, 3, 0, True)
    tail_send(1, 3, 1, True)
    weight_grads(units - 3)
    for k in (2, 1):
        for hh in ((1, 0), (0, 1)):
            for way in range(2):
                tail_send(way, k, hh[way], True)
        weight_grads(units - k)
    for hh in range(2):
        for way in range(2):
            arrive(("t", way, 1, hh), tail_r.at[way, 0, hh])

    def summed(hh):
        return block_of(hh, z) + (unpack(tail_r[0, 0, hh]) + unpack(tail_r[1, 0, hh]))

    tail_h[0] = pack(summed(1 - h))
    send(("twin",), tail_h.at[0], tail_h.at[1], twin)
    mine = summed(h)
    arrive(("twin",), tail_h.at[1])
    grad_in[...] = (mine + unpack(tail_h[1])).astype(BF)

    for copy in sent:
        copy.wait_send()
    for copy in writes:
        copy.wait()


def hand_over(*refs):
    srcs, dsts, held, sem = refs[:4], refs[4:8], refs[8:12], refs[12]
    moves = []
    for i in range(4):
        pieces = 4 if i > 0 else 1
        rows = srcs[i].shape[0] // pieces
        for j in range(pieces):
            at = pl.ds(j * rows, rows)
            moves.append((
                pltpu.make_async_copy(srcs[i].at[at], held[i].at[at], sem.at[0, i, j]),
                pltpu.make_async_copy(held[i].at[at], dsts[i].at[at], sem.at[1, i, j]),
            ))
    for get, _ in moves:
        get.start()
    for get, put in moves:
        get.wait()
        put.start()
    for _, put in moves:
        put.wait()


def body(stored, row_scale, out_grad, gate_weight, up_weight, down_weight):
    tokens, depth = stored.shape
    width = gate_weight.shape[1]
    units = width // 256
    narrow = (112, depth // 2)
    everything = tokens * 16
    anywhere, vmem = pl.BlockSpec(memory_space=pl.ANY), pl.BlockSpec(memory_space=pltpu.VMEM)
    dma = pltpu.SemaphoreType.DMA
    grads = pl.pallas_call(
        kernel,
        out_shape=(
            jax.ShapeDtypeStruct((tokens, depth), BF),
            jax.ShapeDtypeStruct((depth, width), BF),
            jax.ShapeDtypeStruct((depth, width), BF),
            jax.ShapeDtypeStruct((width, depth), BF),
        ),
        in_specs=[vmem, vmem, vmem, anywhere, anywhere, anywhere],
        out_specs=(vmem, anywhere, anywhere, anywhere),
        scratch_shapes=[
            pltpu.VMEM((2, 16, *narrow), BF),
            pltpu.VMEM((2, 16, *narrow), BF),
            pltpu.VMEM((2, everything, depth), BF),
            pltpu.VMEM((2, everything, depth), BF),
            pltpu.VMEM((depth, everything), BF),
            pltpu.VMEM((units, 128, depth), BF),
            pltpu.VMEM((units, depth, 256), BF),
            pltpu.VMEM((units, 128, depth), BF),
            pltpu.VMEM((depth, width), BF),
            pltpu.VMEM((depth, width), BF),
            pltpu.VMEM((units, 8, 112, 384), F32),
            pltpu.VMEM((units, 7, 112, 384), BF),
            pltpu.VMEM((units, 7, 112, 384), BF),
            pltpu.VMEM((units, 2, 8, 112, 384), BF),
            pltpu.VMEM((units, depth, 256), BF),
            pltpu.VMEM((units, depth, 256), BF),
            pltpu.VMEM((units, 256, depth), BF),
            pltpu.VMEM((everything, depth), F32),
            pltpu.VMEM((2, 4, 2, *narrow), BF),
            pltpu.VMEM((2, 4, 2, *narrow), BF),
            pltpu.VMEM((2, *narrow), BF),
            dma((COPIES,)),
            dma((COPIES,)),
            dma((60,)),
        ],
        compiler_params=pltpu.CompilerParams(
            collective_id=0, has_side_effects=True, vmem_limit_bytes=62 * 2**20
        ),
        cost_estimate=pl.CostEstimate(
            flops=16 * everything * depth * width, bytes_accessed=12 * depth * width, transcendentals=0
        ),
    )(stored, row_scale[None, :], out_grad, gate_weight, up_weight, down_weight)
    return pl.pallas_call(
        hand_over,
        out_shape=tuple(jax.ShapeDtypeStruct(g.shape, g.dtype) for g in grads),
        in_specs=[anywhere] * 4,
        out_specs=(anywhere,) * 4,
        scratch_shapes=[pltpu.VMEM(g.shape, g.dtype) for g in grads] + [dma((2, 4, 4))],
        compiler_params=pltpu.CompilerParams(vmem_limit_bytes=62 * 2**20),
    )(*grads)


def solution(mesh):
    placed = (
        P("tensor", "dp"),
        P("tensor"),
        P("tensor", "dp"),
        P("dp", "tensor"),
        P("dp", "tensor"),
        P("tensor", "dp"),
    )
    return jax.shard_map(
        body,
        mesh=mesh,
        in_specs=placed,
        out_specs=(P("tensor", "dp"), P("dp", "tensor"), P("dp", "tensor"), P("tensor", "dp")),
        check_vma=False,
    )
```
